32 devices in a mesh: ens: 4 (over z), rep: 8 (over y, x, core).
Axes of the slice: x: 2, y: 2, z: 4, core: 2. Of those that a mesh axis runs over, the one named last changes fastest.
Arguments:
- cur_states: bfloat16 [8192, 4096], P('rep'), may hold values from -6 to 6
- buffer: bfloat16 [2048, 4096], P('rep'), may hold values from -6 to 6
- fetch_rows: int32 [8, 8, 128], P('rep'), may hold values from 0 to 255
- fetch_counts: int32 [8, 8], replicated, may hold values from 1 to 128, as said below
- actions: int32 [8192], P('rep'), may hold values from 0 to 255
- rewards: float32 [8192], P('rep'), may hold values from -0.5 to 0.5
- terminal: int32 [8192], P('rep'), may hold values 0 or 1
- mc_return: float32 [8192], P('rep'), may hold values from 0 to 1
- w_in: bfloat16 [4, 4096, 512], P('ens'), may hold values from -0.09375 to 0.09375
- w_out: bfloat16 [4, 512, 256], P('ens'), may hold values from -0.25 to 0.25
Outputs:
- targets: float32 [8192], P('rep')
- grad_in: float32 [4, 4096, 512], P('ens', 'rep')
- grad_out: float32 [4, 512, 256], P('ens', 'rep')
The draws below stay inside these ranges and needn't reach their ends.
Inputs may be any that keep to these rules, and one draw needn't show every extreme that they name: `fetch_rows`: each entry indexes the owner's own rows. `fetch_counts`: entry [o, r] is how many leading slots of requester r at owner o are used; some entry equals 128 in every draw.
All inputs are finite; a program needn't handle non-finite values. No bound on the sum of `terminal` on one device may be relied on, other than what follows from the above.
Results may differ from the reference program's by a relative error of at most 0.0044.
Values may be sent and summed in bfloat16 or wider, within the bound.
A program may use at most 192 MiB of HBM per device.

```python
import jax
import jax.numpy as jnp
from jax import lax

D = 4096
HEAD = 512
BINS = 256
CAP = 128
BUF_DEV = 256
MEMBERS = 4
OWNERS = 8
TRANS_ALL = 8192


def draw_fetch_counts(key, part):
    key_counts, key_owner = jax.random.split(jax.random.fold_in(key, 7))
    requester = jnp.arange(OWNERS, dtype=jnp.int32)
    upper = CAP // 3 + (CAP - CAP // 3) * requester // max(OWNERS - 1, 1)
    random_bits = jax.random.randint(key_counts, (OWNERS, OWNERS), 0, 1 << 20)
    counts = 1 + random_bits % upper[None, :]
    chosen_owner = jax.random.randint(key_owner, (), 0, OWNERS)
    owner_ids = jnp.arange(OWNERS, dtype=jnp.int32)[:, None]
    counts = jnp.where((owner_ids == chosen_owner) & (requester[None, :] == OWNERS - 1), CAP, counts)
    return counts.astype(jnp.int32)


def place_ends(drawn, rng, smallest, largest):
    shape = drawn.shape
    place = [jax.random.randint(jax.random.fold_in(rng, axis), (), 0, shape[axis]) for axis in range(len(shape))]
    drawn = drawn.at[tuple(place)].set(smallest)
    longest = shape.index(max(shape))
    place[longest] = (place[longest] + 1) % shape[longest]
    return drawn.at[tuple(place)].set(largest)


def levels(rng, dims, shards, smallest, largest):
    loudness, own = 1.0, jax.random.fold_in(rng, 6)
    for position, shards_of in shards:
        heights = jnp.exp(jax.random.uniform(jax.random.fold_in(own, position), (shards_of,), jnp.float32, smallest / len(shards), largest / len(shards)))
        loudness = loudness * jnp.repeat(heights, dims[position] // shards_of).reshape([-1 if axis == position else 1 for axis in range(len(dims))])
    return loudness


def gaussian(rng, shape, width, reach, pieces=(), held_as=jnp.bfloat16):
    array = width * jax.random.normal(rng, shape, jnp.float32)
    if pieces:
        array = array * levels(rng, shape, pieces, -0.22, 0.18)
    return jnp.clip(array, -reach, reach).astype(held_as)


def setup_inputs(seed: int = 0) -> dict:
    streams_of = jax.random.split(jax.random.key(seed), 11)
    cur_states = gaussian(streams_of[0], (TRANS_ALL, D), 1.0, 6.0, ((0, 8),))
    buffer = gaussian(streams_of[1], (BUF_DEV * OWNERS, D), 1.0, 6.0, ((0, 8),))
    fetch_rows = place_ends(jax.random.randint(streams_of[2], (OWNERS, OWNERS, CAP), 0, BUF_DEV), jax.random.fold_in(streams_of[2], 1), 0, BUF_DEV - 1).astype(jnp.int32)
    fetch_counts = draw_fetch_counts(jax.random.fold_in(streams_of[10], 71), 0)
    actions = place_ends(jax.random.randint(streams_of[4], (TRANS_ALL,), 0, BINS), jax.random.fold_in(streams_of[4], 1), 0, BINS - 1).astype(jnp.int32)
    rewards = jnp.clip(jax.random.uniform(streams_of[5], (TRANS_ALL,), jnp.float32, -0.5, 0.5) * levels(streams_of[5], (TRANS_ALL,), ((0, 8),), -0.4, 0.0), -0.5, 0.5)
    terminal = place_ends((jax.random.randint(streams_of[6], (TRANS_ALL,), 0, 4) < 1).astype(jnp.int32), jax.random.fold_in(streams_of[6], 1), 0, 1)
    mc_return = jnp.clip(1.0 * jax.random.uniform(streams_of[7], (TRANS_ALL,), jnp.float32) ** levels(streams_of[7], (TRANS_ALL,), ((0, 8),), -0.2, 0.2), 0.0, 1.0)
    w_in = gaussian(streams_of[8], (MEMBERS, D, HEAD), D ** -0.5, 0.09375, ((0, 4),))
    w_out = gaussian(streams_of[9], (MEMBERS, HEAD, BINS), HEAD ** -0.5, 0.25, ((0, 4),))
    return dict(cur_states=cur_states, buffer=buffer, fetch_rows=fetch_rows, fetch_counts=fetch_counts, actions=actions, rewards=rewards, terminal=terminal, mc_return=mc_return, w_in=w_in, w_out=w_out)


def critic_head(features, w_first, w_second):
    preact = jnp.dot(features, w_first, preferred_element_type=jnp.float32)
    sigmoid_pre = jax.nn.sigmoid(preact)
    hidden = (preact * sigmoid_pre).astype(jnp.bfloat16)
    values = jax.nn.sigmoid(jnp.dot(hidden, w_second, preferred_element_type=jnp.float32))
    return preact, sigmoid_pre, hidden, values


def reference(cur_states, buffer, fetch_rows, fetch_counts, actions, rewards, terminal, mc_return, w_in, w_out):
    owner_ids = jnp.arange(OWNERS, dtype=jnp.int32)
    positions = (owner_ids[:, None, None] * BUF_DEV + fetch_rows).astype(jnp.int32)
    positions = jnp.transpose(positions, (1, 0, 2)).reshape(-1)
    slot_ids = jnp.arange(CAP, dtype=jnp.int32)
    used = (slot_ids[None, None, :] < jnp.transpose(fetch_counts)[:, :, None]).reshape(-1).astype(jnp.float32)
    counted = jnp.sum(fetch_counts).astype(jnp.float32)
    upcoming = jnp.take(buffer, positions, axis=0)

    def next_best(weights):
        return jnp.max(critic_head(upcoming, weights[0], weights[1])[3], axis=1)

    best_next = lax.map(next_best, (w_in, w_out))
    ens_floor = jnp.min(best_next, axis=0)
    bootstrap = jnp.maximum(ens_floor, mc_return)
    target = rewards + 0.98 * (1.0 - terminal.astype(jnp.float32)) * bootstrap
    targets = used * target
    chosen = actions[:, None] == jnp.arange(BINS, dtype=jnp.int32)[None, :]

    def member_grads(weights):
        w_first, w_second = weights
        preact, sigmoid_pre, hidden, values = critic_head(cur_states, w_first, w_second)
        taken = jnp.sum(jnp.where(chosen, values, 0.0), axis=1)
        errors = used * 2.0 * (taken - target) * taken * (1.0 - taken) * (65536.0 / counted)
        d_logits = jnp.where(chosen, errors[:, None], 0.0).astype(jnp.bfloat16)
        grad_second = lax.dot_general(hidden, d_logits, (((0,), (0,)), ((), ())), preferred_element_type=jnp.float32)
        back = lax.dot_general(d_logits, w_second, (((1,), (1,)), ((), ())), preferred_element_type=jnp.float32)
        d_hidden = (back * sigmoid_pre * (1.0 + preact * (1.0 - sigmoid_pre))).astype(jnp.bfloat16)
        grad_first = lax.dot_general(cur_states, d_hidden, (((0,), (0,)), ((), ())), preferred_element_type=jnp.float32)
        return grad_first, grad_second

    grad_in, grad_out = lax.map(member_grads, (w_in, w_out))
    return targets, grad_in, grad_out
```

```python
import functools

import jax
import jax.numpy as jnp
from jax import lax
from jax.experimental import pallas as pl
from jax.experimental.pallas import tpu as pltpu
from jax.sharding import PartitionSpec as P

F32 = jnp.float32
BF16 = jnp.bfloat16
MESH = pl.DeviceIdType.MESH


def flip(value, bits, size):
    out, base = 0, 1
    while base < size:
        out = out + ((value // base + (bits // base) % 2) % 2) * base
        base *= 2
    return out


def kernel(
    n, members, tile,
    cur_hbm, buf_hbm, fetch_ref, counts_ref, act_ref, rew_ref, term_ref, mc_ref, win_hbm, wout_ref,
    tgt_ref, gin_ref, gout_ref,
    cur, buf, win, wout_t, hid, slope_t, tk, dh_t, gout, mine, ens_got, serve, got,
    own, core_src, core_got, chip_src, chip_got,
    in_sem, cur_sem, ens_ss, ens_rs, rep_ss, rep_rs, core_ss, core_rs, chip_ss, chip_rs,
):
    me, member = lax.axis_index("rep"), lax.axis_index("ens")
    slots, width = cur.shape
    head, bins = wout_ref.shape
    cap = fetch_ref.shape[1]
    rows = buf.shape[0]
    tiles = slots // tile
    chips = n // 2
    chip, core = me // 2, me % 2
    share = width // n
    side = share // bins
    half = head // n // side

    load_win = pltpu.make_async_copy(win_hbm, win, in_sem.at[0])
    load_buf = pltpu.make_async_copy(buf_hbm, buf, in_sem.at[1])
    load_win.start()
    load_buf.start()

    def load_cur(i):
        part = pl.ds(pl.multiple_of(i * tile, tile), tile)
        return pltpu.make_async_copy(cur_hbm.at[part], cur.at[part], cur_sem.at[i])

    for i in range(tiles):
        load_cur(i).start()

    barrier = pltpu.get_barrier_semaphore()
    for d in range(1, members):
        pl.semaphore_signal(barrier, inc=1, device_id={"ens": (member + d) % members}, device_id_type=MESH)
    for d in range(1, n):
        pl.semaphore_signal(barrier, inc=1, device_id={"rep": (me + d) % n}, device_id_type=MESH)

    wout_t[...] = wout_ref[...].astype(F32).T.astype(BF16)
    counted = jnp.int32(0)
    for a in range(n):
        for b in range(n):
            counted = counted + counts_ref[a, b]
    gain = 65536.0 / jnp.full((1, cap), counted, jnp.int32).astype(F32)

    def logits_of(hidden):
        return lax.dot_general(
            wout_t[...], hidden, (((1,), (1,)), ((), ())), preferred_element_type=F32
        )

    load_win.wait()
    load_buf.wait()
    pre = jnp.dot(buf[...], win[...], preferred_element_type=F32)
    hidden = (pre * jax.nn.sigmoid(pre)).astype(BF16)
    best = jnp.max(logits_of(hidden), axis=0, keepdims=True)
    mine[...] = jnp.broadcast_to(best, mine.shape)
    pl.semaphore_wait(barrier, members - 1 + n - 1)

    def ens_copy(d):
        return pltpu.make_async_remote_copy(
            src_ref=mine, dst_ref=ens_got.at[d - 1], send_sem=ens_ss.at[d - 1], recv_sem=ens_rs.at[d - 1],
            device_id={"ens": (member + d) % members}, device_id_type=MESH,
        )

    for d in range(1, members):
        ens_copy(d).start()

    def forward(i, carry):
        load_cur(i).wait()
        part = pl.ds(pl.multiple_of(i * tile, tile), tile)
        pre = jnp.dot(cur[part, :], win[...], preferred_element_type=F32)
        sig = jax.nn.sigmoid(pre)
        hidden = (pre * sig).astype(BF16)
        hid[part, :] = hidden
        slope_t[:, part] = (sig * (1.0 + pre * (1.0 - sig))).T
        logits = logits_of(hidden)
        chosen = lax.broadcasted_iota(jnp.int32, (bins, tile), 0) == act_ref[0:1, part]
        tk[0:1, part] = jnp.sum(jnp.where(chosen, logits, 0.0), axis=0, keepdims=True)
        return carry

    lax.fori_loop(0, tiles // 2, forward, 0)

    floor = mine[0:1, :]
    for d in range(1, members):
        ens_copy(d).wait()
        floor = jnp.minimum(floor, ens_got[d - 1, 0:1, :])
    eye = lax.broadcasted_iota(jnp.int32, (rows, rows), 0) == lax.broadcasted_iota(jnp.int32, (rows, rows), 1)
    floor_col = jnp.sum(jnp.where(eye, jnp.broadcast_to(floor, (rows, rows)), 0.0), axis=1, keepdims=True)
    row_ids = lax.broadcasted_iota(jnp.int32, (rows, cap), 0)
    for r in range(n):
        hit = row_ids == fetch_ref[r:r + 1, :]
        served = jnp.sum(jnp.where(hit, jnp.broadcast_to(floor_col, (rows, cap)), 0.0), axis=0, keepdims=True)
        serve[r] = jnp.broadcast_to(served, serve.shape[1:])

    def rep_copy(d, slot):
        dst = (me + d) % n
        return pltpu.make_async_remote_copy(
            src_ref=serve.at[dst], dst_ref=got.at[slot], send_sem=rep_ss.at[d - 1], recv_sem=rep_rs.at[slot],
            device_id={"rep": dst}, device_id_type=MESH,
        )

    for d in range(1, n):
        rep_copy(d, me).start()
    got[me] = serve[me]

    lax.fori_loop(tiles // 2, tiles, forward, 0)

    for d in range(1, n):
        rep_copy(d, (me + n - d) % n).wait_recv()
    place = lax.broadcasted_iota(jnp.int32, (1, cap), 1)
    bin_ids = lax.broadcasted_iota(jnp.int32, (bins, cap), 0)
    pieces = []
    for o in range(n):
        part = slice(o * cap, (o + 1) * cap)
        used = jnp.where(place < counts_ref[o, me], 1.0, 0.0)
        bootstrap = jnp.maximum(jax.nn.sigmoid(got[o, 0:1, :]), mc_ref[0:1, part])
        target = rew_ref[0:1, part] + 0.98 * (1.0 - term_ref[0:1, part].astype(F32)) * bootstrap
        tgt_ref[0:1, part] = used * target
        taken = jax.nn.sigmoid(tk[0:1, part])
        errors = used * 2.0 * (taken - target) * taken * (1.0 - taken) * gain
        pieces.append(jnp.where(bin_ids == act_ref[0:1, part], errors, 0.0).astype(BF16))
    d_logits_t = jnp.concatenate(pieces, axis=1)
    back_t = jnp.dot(wout_ref[...], d_logits_t, preferred_element_type=F32)
    dh_t[...] = (back_t * slope_t[...]).astype(BF16)
    gout[...] = jnp.dot(d_logits_t, hid[...], preferred_element_type=F32).T

    def grad_of(k):
        cols = pl.ds(pl.multiple_of(k * share, share), share)
        return jnp.dot(dh_t[...], cur[:, cols], preferred_element_type=F32)

    def out_rows(k, j):
        return gout[pl.ds(pl.multiple_of(k * (half * side) + j * half, half), half), :]

    def core_copy(s):
        return pltpu.make_async_remote_copy(
            src_ref=core_src.at[s], dst_ref=core_got.at[s], send_sem=core_ss.at[s], recv_sem=core_rs.at[s],
            device_id={"rep": chip * 2 + 1 - core}, device_id_type=MESH,
        )

    def chip_copy(s, there):
        return pltpu.make_async_remote_copy(
            src_ref=chip_src.at[s], dst_ref=chip_got.at[s], send_sem=chip_ss.at[s], recv_sem=chip_rs.at[s],
            device_id={"rep": there * 2 + core}, device_id_type=MESH,
        )

    order = [flip(chip, d, chips) for d in range(chips - 1, -1, -1)]

    def forward_sum(s):
        core_copy(s).wait()
        if s < chips - 1:
            chip_src[s] = (own[s] + core_got[s].astype(F32)).astype(BF16)
            chip_copy(s, order[s]).start()

    for s in range(chips):
        other, mine_k = order[s] * 2 + 1 - core, order[s] * 2 + core
        core_src[s, 0:head, :] = grad_of(other).astype(BF16)
        for j in range(side):
            core_src[s, head:head + half, j * bins:(j + 1) * bins] = out_rows(other, j).astype(BF16)
        core_copy(s).start()
        own[s, 0:head, :] = grad_of(mine_k)
        for j in range(side):
            own[s, head:head + half, j * bins:(j + 1) * bins] = out_rows(mine_k, j)
        if s > 0:
            forward_sum(s - 1)
    forward_sum(chips - 1)

    total = own[chips - 1] + core_got[chips - 1].astype(F32)
    for s in range(chips - 1):
        chip_copy(s, order[s]).wait()
        total = total + chip_got[s].astype(F32)
    gin_ref[...] = total[0:head, :].T
    for j in range(side):
        gout_ref[j * half:(j + 1) * half, :] = total[head:head + half, j * bins:(j + 1) * bins]
    for d in range(1, n):
        rep_copy(d, me).wait_send()


def shards(
    members, n,
    cur_states, buffer, fetch_rows, fetch_counts, actions, rewards, terminal, mc_return, w_in, w_out
):
    slots, width = cur_states.shape
    rows = buffer.shape[0]
    head, bins = w_out.shape[1:]
    cap = fetch_rows.shape[2]
    chips = n // 2
    share = width // n
    tile = min(256, slots // 2)
    packed = head + head // n // (share // bins)
    vmem, hbm = pl.BlockSpec(memory_space=pltpu.VMEM), pl.BlockSpec(memory_space=pl.ANY)
    dma = pltpu.SemaphoreType.DMA
    targets, grad_first, grad_second = pl.pallas_call(
        functools.partial(kernel, n, members, tile),
        out_shape=(
            jax.ShapeDtypeStruct((1, slots), F32),
            jax.ShapeDtypeStruct((share, head), F32),
            jax.ShapeDtypeStruct((head // n, bins), F32),
        ),
        in_specs=[hbm, hbm, vmem, pl.BlockSpec(memory_space=pltpu.SMEM), vmem, vmem, vmem, vmem, hbm, vmem],
        out_specs=(vmem, vmem, vmem),
        scratch_shapes=[
            pltpu.VMEM((slots, width), BF16),
            pltpu.VMEM((rows, width), BF16),
            pltpu.VMEM((width, head), BF16),
            pltpu.VMEM((bins, head), BF16),
            pltpu.VMEM((slots, head), BF16),
            pltpu.VMEM((head, slots), F32),
            pltpu.VMEM((8, slots), F32),
            pltpu.VMEM((head, slots), BF16),
            pltpu.VMEM((head, bins), F32),
            pltpu.VMEM((8, rows), F32),
            pltpu.VMEM((members - 1, 8, rows), F32),
            pltpu.VMEM((n, 8, cap), F32),
            pltpu.VMEM((n, 8, cap), F32),
            pltpu.VMEM((chips, packed, share), F32),
            pltpu.VMEM((chips, packed, share), BF16),
            pltpu.VMEM((chips, packed, share), BF16),
            pltpu.VMEM((chips - 1, packed, share), BF16),
            pltpu.VMEM((chips - 1, packed, share), BF16),
            dma((2,)), dma((slots // tile,)),
            dma((members - 1,)), dma((members - 1,)),
            dma((n - 1,)), dma((n,)),
            dma((chips,)), dma((chips,)),
            dma((chips - 1,)), dma((chips - 1,)),
        ],
        compiler_params=pltpu.CompilerParams(
            collective_id=0, has_side_effects=True, vmem_limit_bytes=60 * 1024 * 1024
        ),
    )(
        cur_states, buffer, fetch_rows[0], fetch_counts,
        actions.reshape(1, slots), rewards.reshape(1, slots), terminal.reshape(1, slots), mc_return.reshape(1, slots),
        w_in[0], w_out[0],
    )
    return targets.reshape(slots), grad_first[None], grad_second[None]


def solution(mesh):
    placed = (
        P("rep", None),
        P("rep", None),
        P("rep", None, None),
        P(),
        P("rep"),
        P("rep"),
        P("rep"),
        P("rep"),
        P("ens", None, None),
        P("ens", None, None),
    )
    return jax.shard_map(
        functools.partial(shards, mesh.shape["ens"], mesh.shape["rep"]),
        mesh=mesh,
        in_specs=placed,
        out_specs=(P("rep"), P("ens", "rep", None), P("ens", "rep", None)),
        check_vma=False,
    )
```

```python
import functools

import jax
import jax.numpy as jnp
from jax import lax
from jax.experimental import pallas as pl
from jax.experimental.pallas import tpu as pltpu
from jax.sharding import PartitionSpec as P

F32 = jnp.float32
BF16 = jnp.bfloat16
MESH = pl.DeviceIdType.MESH


def flip(value, bits, size):
    out, base = 0, 1
    while base < size:
        out = out + ((value // base + (bits // base) % 2) % 2) * base
        base *= 2
    return out


def kernel(
    n, members, tile, parts,
    cur_hbm, buf_hbm, fetch_ref, counts_ref, act_ref, rew_ref, term_ref, mc_ref, win_hbm, wout_ref,
    tgt_ref, tot_ref,
    cur, buf, win, wout_t, hid, slope_t, tk, dh_t, gout, mine, ens_got, serve, got,
    own, core_src, core_got, chip_src, chip_got,
    in_sem, cur_sem, ens_ss, ens_rs, rep_ss, rep_rs, core_ss, core_rs, chip_ss, chip_rs,
):
    me, member = lax.axis_index("rep"), lax.axis_index("ens")
    slots, width = cur.shape
    head, bins = wout_ref.shape
    cap = fetch_ref.shape[1]
    rows = buf.shape[0]
    tiles = slots // tile
    chips = n // 2
    chip, core = me // 2, me % 2
    share = width // n
    side = share // bins
    upper, lower = head // 2, head // n // (2 * side)
    steps, relay = steps_of(chips)

    def relayed(d):
        return relay and d == 3

    depth = width // parts

    def load_win(k):
        part = slice(k * depth, (k + 1) * depth)
        return pltpu.make_async_copy(win_hbm.at[part], win.at[part], in_sem.at[2 * k])

    def load_buf(k):
        part = slice(k * depth, (k + 1) * depth)
        return pltpu.make_async_copy(buf_hbm.at[:, part], buf.at[:, part], in_sem.at[2 * k + 1])

    for k in range(parts):
        load_win(k).start()
        load_buf(k).start()

    def load_cur(i):
        part = pl.ds(pl.multiple_of(i * tile, tile), tile)
        return pltpu.make_async_copy(cur_hbm.at[part], cur.at[part], cur_sem.at[i])

    barrier = pltpu.get_barrier_semaphore()
    for d in range(1, members):
        pl.semaphore_signal(barrier, inc=1, device_id={"ens": (member + d) % members}, device_id_type=MESH)
    for d in range(1, n):
        pl.semaphore_signal(barrier, inc=1, device_id={"rep": (me + d) % n}, device_id_type=MESH)

    wout_t[...] = wout_ref[...].astype(F32).T.astype(BF16)
    counted = jnp.int32(0)
    for a in range(n):
        for b in range(n):
            counted = counted + counts_ref[a, b]
    gain = 65536.0 / jnp.full((1, cap), counted, jnp.int32).astype(F32)

    def logits_of(hidden):
        return lax.dot_general(
            wout_t[...], hidden, (((1,), (1,)), ((), ())), preferred_element_type=F32
        )

    pre = None
    for k in range(parts):
        load_win(k).wait()
        load_buf(k).wait()
        if k == min(1, parts - 1):
            for i in range(tiles):
                load_cur(i).start()
        part = slice(k * depth, (k + 1) * depth)
        term = jnp.dot(buf[:, part], win[part, :], preferred_element_type=F32)
        pre = term if pre is None else pre + term
    hidden = (pre * jax.nn.sigmoid(pre)).astype(BF16)
    best = jnp.max(logits_of(hidden), axis=0, keepdims=True)
    mine[...] = jnp.broadcast_to(best, mine.shape)
    pl.semaphore_wait(barrier, members - 1 + n - 1)

    def ens_copy(d):
        return pltpu.make_async_remote_copy(
            src_ref=mine, dst_ref=ens_got.at[d - 1], send_sem=ens_ss.at[d - 1], recv_sem=ens_rs.at[d - 1],
            device_id={"ens": (member + d) % members}, device_id_type=MESH,
        )

    for d in range(1, members):
        ens_copy(d).start()

    def forward(i, carry):
        load_cur(i).wait()
        part = pl.ds(pl.multiple_of(i * tile, tile), tile)
        pre = jnp.dot(cur[part, :], win[...], preferred_element_type=F32)
        sig = jax.nn.sigmoid(pre)
        hidden = (pre * sig).astype(BF16)
        hid[part, :] = hidden
        slope_t[:, part] = (sig * (1.0 + pre * (1.0 - sig))).T
        logits = logits_of(hidden)
        chosen = lax.broadcasted_iota(jnp.int32, (bins, tile), 0) == act_ref[0:1, part]
        tk[0:1, part] = jnp.sum(jnp.where(chosen, logits, 0.0), axis=0, keepdims=True)
        return carry

    lax.fori_loop(0, tiles // 2, forward, 0)

    floor = mine[0:1, :]
    for d in range(1, members):
        ens_copy(d).wait()
        floor = jnp.minimum(floor, ens_got[d - 1, 0:1, :])
    eye = lax.broadcasted_iota(jnp.int32, (rows, rows), 0) == lax.broadcasted_iota(jnp.int32, (rows, rows), 1)
    floor_col = jnp.sum(jnp.where(eye, jnp.broadcast_to(floor, (rows, rows)), 0.0), axis=1, keepdims=True)
    row_ids = lax.broadcasted_iota(jnp.int32, (rows, cap), 0)
    for r in range(n):
        hit = row_ids == fetch_ref[r:r + 1, :]
        served = jnp.sum(jnp.where(hit, jnp.broadcast_to(floor_col, (rows, cap)), 0.0), axis=0, keepdims=True)
        serve[r] = jnp.broadcast_to(served, serve.shape[1:])

    def rep_copy(d, slot):
        dst = (me + d) % n
        return pltpu.make_async_remote_copy(
            src_ref=serve.at[dst], dst_ref=got.at[slot], send_sem=rep_ss.at[d - 1], recv_sem=rep_rs.at[slot],
            device_id={"rep": dst}, device_id_type=MESH,
        )

    for d in range(1, n):
        rep_copy(d, me).start()
    got[me] = serve[me]

    lax.fori_loop(tiles // 2, tiles, forward, 0)

    for d in range(1, n):
        rep_copy(d, (me + n - d) % n).wait_recv()
    place = lax.broadcasted_iota(jnp.int32, (1, cap), 1)
    bin_ids = lax.broadcasted_iota(jnp.int32, (bins, cap), 0)
    pieces = []
    for o in range(n):
        part = slice(o * cap, (o + 1) * cap)
        used = jnp.where(place < counts_ref[o, me], 1.0, 0.0)
        bootstrap = jnp.maximum(jax.nn.sigmoid(got[o, 0:1, :]), mc_ref[0:1, part])
        target = rew_ref[0:1, part] + 0.98 * (1.0 - term_ref[0:1, part].astype(F32)) * bootstrap
        tgt_ref[0:1, part] = used * target
        taken = jax.nn.sigmoid(tk[0:1, part])
        errors = used * 2.0 * (taken - target) * taken * (1.0 - taken) * gain
        pieces.append(jnp.where(bin_ids == act_ref[0:1, part], errors, 0.0).astype(BF16))
    d_logits_t = jnp.concatenate(pieces, axis=1)
    back_t = jnp.dot(wout_ref[...], d_logits_t, preferred_element_type=F32)
    dh_t[...] = (back_t * slope_t[...]).astype(BF16)
    gout[...] = jnp.dot(d_logits_t, hid[...], preferred_element_type=F32).T

    def grad_of(k, p):
        cols = pl.ds(pl.multiple_of(k * share, share), share)
        return jnp.dot(dh_t[p * upper:(p + 1) * upper, :], cur[:, cols], preferred_element_type=F32)

    def out_rows(k, p, j):
        first = k * (2 * side * lower) + (p * side + j) * lower
        return gout[pl.ds(pl.multiple_of(first, lower), lower), :]

    def core_copy(i):
        return pltpu.make_async_remote_copy(
            src_ref=core_src.at[i], dst_ref=core_got.at[i], send_sem=core_ss.at[i], recv_sem=core_rs.at[i],
            device_id={"rep": chip * 2 + 1 - core}, device_id_type=MESH,
        )

    def chip_copy(i):
        d, p = steps[i]
        there = flip(chip, p + 1 if relayed(d) else d, chips)
        return pltpu.make_async_remote_copy(
            src_ref=chip_src.at[i], dst_ref=chip_got.at[i], send_sem=chip_ss.at[i], recv_sem=chip_rs.at[i],
            device_id={"rep": there * 2 + core}, device_id_type=MESH,
        )

    def compute(i):
        d, p = steps[i]
        there = flip(chip, d, chips)
        for k, dst in ((there * 2 + 1 - core, core_src), (there * 2 + core, own)):
            dst[i, 0:upper, :] = grad_of(k, p).astype(dst.dtype)
            for j in range(side):
                dst[i, upper:upper + lower, j * bins:(j + 1) * bins] = out_rows(k, p, j).astype(dst.dtype)
            if dst is core_src:
                core_copy(i).start()

    def pass_on(i):
        d, p = steps[i]
        core_copy(i).wait()
        value = own[i] + core_got[i].astype(F32)
        if d == 0:
            own[i] = value
            return
        if relay and (d, p) in ((1, 1), (2, 0)):
            came = steps.index((3, p))
            chip_copy(came).wait_recv()
            value = value + chip_got[came].astype(F32)
        chip_src[i] = value.astype(BF16)
        chip_copy(i).start()

    last = len(steps) - 1
    late = [i for i in range(last + 1) if relay and steps[i] in ((1, 1), (2, 0))]
    for i in range(last + 1):
        compute(i)
        if i > 0 and i - 1 not in late:
            pass_on(i - 1)
    pass_on(last)
    for i in late:
        pass_on(i)

    for i in range(last - 1):
        d, p = steps[i]
        if relayed(d):
            chip_copy(i).wait_send()
            continue
        chip_copy(i).wait()
        if i not in late:
            own[last - 1 + p] = own[last - 1 + p] + chip_got[i].astype(F32)
    for p in range(2):
        total = own[last - 1 + p]
        for i in late:
            if steps[i][1] == p:
                total = total + chip_got[i].astype(F32)
        tot_ref[p] = total
    for d in range(1, n):
        rep_copy(d, me).wait_send()


def steps_of(chips):
    if chips == 4:
        return [(3, 0), (3, 1), (1, 0), (2, 1), (1, 1), (2, 0), (0, 0), (0, 1)], True
    return [(d, p) for d in range(chips - 1, -1, -1) for p in range(2)], False


def unpack(side, tgt_in, tot, tgt_ref, gin_ref, gout_ref):
    upper, lower = gin_ref.shape[1] // 2, gout_ref.shape[0] // (2 * side)
    bins = gout_ref.shape[1]
    tgt_ref[...] = tgt_in[...]
    for p in range(2):
        gin_ref[:, p * upper:(p + 1) * upper] = tot[p, 0:upper, :].T
        for j in range(side):
            first = (p * side + j) * lower
            gout_ref[first:first + lower, :] = tot[p, upper:upper + lower, j * bins:(j + 1) * bins]


def shards(
    members, n,
    cur_states, buffer, fetch_rows, fetch_counts, actions, rewards, terminal, mc_return, w_in, w_out
):
    slots, width = cur_states.shape
    rows = buffer.shape[0]
    head, bins = w_out.shape[1:]
    cap = fetch_rows.shape[2]
    chips = n // 2
    share = width // n
    tile = min(256, slots // 2)
    side = share // bins
    packed = head // 2 + head // n // (2 * side)
    count = len(steps_of(chips)[0])
    parts = 4
    vmem, hbm = pl.BlockSpec(memory_space=pltpu.VMEM), pl.BlockSpec(memory_space=pl.ANY)
    dma = pltpu.SemaphoreType.DMA
    targets, totals = pl.pallas_call(
        functools.partial(kernel, n, members, tile, parts),
        out_shape=(
            jax.ShapeDtypeStruct((1, slots), F32),
            jax.ShapeDtypeStruct((2, packed, share), F32),
        ),
        in_specs=[hbm, hbm, vmem, pl.BlockSpec(memory_space=pltpu.SMEM), vmem, vmem, vmem, vmem, hbm, vmem],
        out_specs=(vmem, vmem),
        scratch_shapes=[
            pltpu.VMEM((slots, width), BF16),
            pltpu.VMEM((rows, width), BF16),
            pltpu.VMEM((width, head), BF16),
            pltpu.VMEM((bins, head), BF16),
            pltpu.VMEM((slots, head), BF16),
            pltpu.VMEM((head, slots), F32),
            pltpu.VMEM((8, slots), F32),
            pltpu.VMEM((head, slots), BF16),
            pltpu.VMEM((head, bins), F32),
            pltpu.VMEM((8, rows), F32),
            pltpu.VMEM((members - 1, 8, rows), F32),
            pltpu.VMEM((n, 8, cap), F32),
            pltpu.VMEM((n, 8, cap), F32),
            pltpu.VMEM((count, packed, share), F32),
            pltpu.VMEM((count, packed, share), BF16),
            pltpu.VMEM((count, packed, share), BF16),
            pltpu.VMEM((count - 2, packed, share), BF16),
            pltpu.VMEM((count - 2, packed, share), BF16),
            dma((2 * parts,)), dma((slots // tile,)),
            dma((members - 1,)), dma((members - 1,)),
            dma((n - 1,)), dma((n,)),
            dma((count,)), dma((count,)),
            dma((count - 2,)), dma((count - 2,)),
        ],
        compiler_params=pltpu.CompilerParams(
            collective_id=0, has_side_effects=True, vmem_limit_bytes=60 * 1024 * 1024
        ),
    )(
        cur_states, buffer, fetch_rows[0], fetch_counts,
        actions.reshape(1, slots), rewards.reshape(1, slots), terminal.reshape(1, slots), mc_return.reshape(1, slots),
        w_in[0], w_out[0],
    )
    targets, grad_first, grad_second = pl.pallas_call(
        functools.partial(unpack, side),
        out_shape=(
            jax.ShapeDtypeStruct((1, slots), F32),
            jax.ShapeDtypeStruct((share, head), F32),
            jax.ShapeDtypeStruct((head // n, bins), F32),
        ),
        in_specs=[vmem, vmem],
        out_specs=(vmem, vmem, vmem),
        compiler_params=pltpu.CompilerParams(vmem_limit_bytes=60 * 1024 * 1024),
    )(targets, totals)
    return targets.reshape(slots), grad_first[None], grad_second[None]


def solution(mesh):
    placed = (
        P("rep", None),
        P("rep", None),
        P("rep", None, None),
        P(),
        P("rep"),
        P("rep"),
        P("rep"),
        P("rep"),
        P("ens", None, None),
        P("ens", None, None),
    )
    return jax.shard_map(
        functools.partial(shards, mesh.shape["ens"], mesh.shape["rep"]),
        mesh=mesh,
        in_specs=placed,
        out_specs=(P("rep"), P("ens", "rep", None), P("ens", "rep", None)),
        check_vma=False,
    )
```

```python
import functools

import jax
import jax.numpy as jnp
from jax import lax
from jax.experimental import pallas as pl
from jax.experimental.pallas import tpu as pltpu
from jax.sharding import PartitionSpec as P

F32 = jnp.float32
BF16 = jnp.bfloat16
MESH = pl.DeviceIdType.MESH


def flip(value, bits, size):
    out, base = 0, 1
    while base < size:
        out = out + ((value // base + (bits // base) % 2) % 2) * base
        base *= 2
    return out


def kernel(
    n, members, first, parts,
    cur_hbm, buf_hbm, fetch_ref, counts_ref, act_ref, rew_ref, term_ref, mc_ref, win_hbm, wout_ref,
    tgt_ref, tot_ref,
    states, pre, win, wout_t, hid, slope_t, tk, dh_t, gout, mine, ens_got, serve, got,
    own, core_src, core_got, chip_src, chip_got,
    in_sem, cur_sem, ens_ss, ens_rs, rep_ss, rep_rs, core_ss, core_rs, chip_ss, chip_rs,
):
    me, member = lax.axis_index("rep"), lax.axis_index("ens")
    head, bins = wout_ref.shape
    cap = fetch_ref.shape[1]
    slots, width = cur_hbm.shape
    rows = buf_hbm.shape[0]
    chips = n // 2
    chip, core = me // 2, me % 2
    share = width // n
    side = share // bins
    upper, lower = head // 2, head // n // side
    steps, relay = steps_of(chips)

    def relayed(d):
        return relay and d == 3

    depth = width // parts

    def load_win(k):
        part = slice(k * depth, (k + 1) * depth)
        return pltpu.make_async_copy(win_hbm.at[part], win.at[part], in_sem.at[2 * k])

    def load_buf(k):
        part = slice(k * depth, (k + 1) * depth)
        return pltpu.make_async_copy(buf_hbm.at[:, part], states.at[0:rows, part], in_sem.at[2 * k + 1])

    def load_early(k):
        part = slice(k * depth, (k + 1) * depth)
        return pltpu.make_async_copy(
            cur_hbm.at[0:first, part], states.at[rows:rows + first, part], cur_sem.at[k]
        )

    load_late = pltpu.make_async_copy(
        cur_hbm.at[first:slots], states.at[rows + first:rows + slots], cur_sem.at[parts]
    )
    for k in range(parts):
        load_win(k).start()
        load_buf(k).start()
        load_early(k).start()

    barrier = pltpu.get_barrier_semaphore()
    for d in range(1, members):
        pl.semaphore_signal(barrier, inc=1, device_id={"ens": (member + d) % members}, device_id_type=MESH)
    for d in range(1, n):
        pl.semaphore_signal(barrier, inc=1, device_id={"rep": (me + d) % n}, device_id_type=MESH)

    wout_t[...] = wout_ref[...].astype(F32).T.astype(BF16)
    counted = jnp.int32(0)
    for a in range(n):
        for b in range(n):
            counted = counted + counts_ref[a, b]
    gain = 65536.0 / jnp.full((1, cap), counted, jnp.int32).astype(F32)

    def activate(begin, end):
        for top in range(begin, end, 128):
            down = slice(top, top + 128)
            for left in range(0, head, 128):
                across = slice(left, left + 128)
                x = pre[down, across]
                sig = jax.nn.sigmoid(x)
                hid[down, across] = (x * sig).astype(BF16)
                if top >= rows:
                    slope_t[across, top - rows:top - rows + 128] = (sig * (1.0 + x * (1.0 - sig))).T

    def logits_of(begin, end):
        return lax.dot_general(
            wout_t[...], hid[begin:end, :], (((1,), (1,)), ((), ())), preferred_element_type=F32
        )

    def take(begin, end):
        logits = logits_of(rows + begin, rows + end)
        ids = lax.broadcasted_iota(jnp.int32, (bins, 128), 0)
        for left in range(0, end - begin, 128):
            part = slice(begin + left, begin + left + 128)
            picked = jnp.where(ids == act_ref[0:1, part], logits[:, left:left + 128], 0.0)
            tk[0:1, part] = jnp.sum(picked, axis=0, keepdims=True)

    for k in range(parts):
        load_win(k).wait()
        load_buf(k).wait()
        load_early(k).wait()
        if k == min(1, parts - 1):
            load_late.start()
        part = slice(k * depth, (k + 1) * depth)
        term = jnp.dot(states[0:rows + first, part], win[part, :], preferred_element_type=F32)
        if k == 0:
            pre[0:rows + first, :] = term
        else:
            pre[0:rows + first, :] += term
    activate(0, rows)
    best = jnp.max(logits_of(0, rows), axis=0, keepdims=True)
    mine[...] = jnp.broadcast_to(best, mine.shape)
    pl.semaphore_wait(barrier, members - 1 + n - 1)

    def ens_copy(d):
        return pltpu.make_async_remote_copy(
            src_ref=mine, dst_ref=ens_got.at[d - 1], send_sem=ens_ss.at[d - 1], recv_sem=ens_rs.at[d - 1],
            device_id={"ens": (member + d) % members}, device_id_type=MESH,
        )

    for d in range(1, members):
        ens_copy(d).start()

    activate(rows, rows + first)
    take(0, first)

    floor = mine[0:1, :]
    for d in range(1, members):
        ens_copy(d).wait()
        floor = jnp.minimum(floor, ens_got[d - 1, 0:1, :])
    eye = lax.broadcasted_iota(jnp.int32, (rows, rows), 0) == lax.broadcasted_iota(jnp.int32, (rows, rows), 1)
    floor_col = jnp.sum(jnp.where(eye, jnp.broadcast_to(floor, (rows, rows)), 0.0), axis=1, keepdims=True)
    row_ids = lax.broadcasted_iota(jnp.int32, (rows, cap), 0)
    for r in range(n):
        hit = row_ids == fetch_ref[r:r + 1, :]
        served = jnp.sum(jnp.where(hit, jnp.broadcast_to(floor_col, (rows, cap)), 0.0), axis=0, keepdims=True)
        serve[r] = jnp.broadcast_to(served, serve.shape[1:])

    def rep_copy(d, slot):
        dst = (me + d) % n
        return pltpu.make_async_remote_copy(
            src_ref=serve.at[dst], dst_ref=got.at[slot], send_sem=rep_ss.at[d - 1], recv_sem=rep_rs.at[slot],
            device_id={"rep": dst}, device_id_type=MESH,
        )

    for d in range(1, n):
        rep_copy(d, me).start()
    got[me] = serve[me]

    load_late.wait()
    pre[rows + first:rows + slots, :] = jnp.dot(
        states[rows + first:rows + slots, :], win[...], preferred_element_type=F32
    )
    activate(rows + first, rows + slots)
    take(first, slots)

    for d in range(1, n):
        rep_copy(d, (me + n - d) % n).wait_recv()
    place = lax.broadcasted_iota(jnp.int32, (1, cap), 1)
    bin_ids = lax.broadcasted_iota(jnp.int32, (bins, cap), 0)
    pieces = []
    for o in range(n):
        part = slice(o * cap, (o + 1) * cap)
        used = jnp.where(place < counts_ref[o, me], 1.0, 0.0)
        bootstrap = jnp.maximum(jax.nn.sigmoid(got[o, 0:1, :]), mc_ref[0:1, part])
        target = rew_ref[0:1, part] + 0.98 * (1.0 - term_ref[0:1, part].astype(F32)) * bootstrap
        tgt_ref[0:1, part] = used * target
        taken = jax.nn.sigmoid(tk[0:1, part])
        errors = used * 2.0 * (taken - target) * taken * (1.0 - taken) * gain
        pieces.append(jnp.where(bin_ids == act_ref[0:1, part], errors, 0.0).astype(BF16))
    d_logits_t = jnp.concatenate(pieces, axis=1)

    def back(p):
        part = slice(p * upper, (p + 1) * upper)
        back_t = jnp.dot(wout_ref[part, :], d_logits_t, preferred_element_type=F32)
        dh_t[part, :] = (back_t * slope_t[part, :]).astype(BF16)

    def grad_of(k, p):
        cols = pl.ds(pl.multiple_of(k * share, share), share)
        return jnp.dot(dh_t[p * upper:(p + 1) * upper, :], states[rows:rows + slots, cols], preferred_element_type=F32)

    def out_rows(k, j):
        return gout[pl.ds(pl.multiple_of((k * side + j) * lower, lower), lower), :]

    def size(i):
        return upper + lower * steps[i][1]

    def core_copy(i):
        return pltpu.make_async_remote_copy(
            src_ref=core_src.at[i, 0:size(i)], dst_ref=core_got.at[i, 0:size(i)], send_sem=core_ss.at[i], recv_sem=core_rs.at[i],
            device_id={"rep": chip * 2 + 1 - core}, device_id_type=MESH,
        )

    def chip_copy(i):
        d, p = steps[i]
        there = flip(chip, p + 1 if relayed(d) else d, chips)
        return pltpu.make_async_remote_copy(
            src_ref=chip_src.at[i, 0:size(i)], dst_ref=chip_got.at[i, 0:size(i)], send_sem=chip_ss.at[i], recv_sem=chip_rs.at[i],
            device_id={"rep": there * 2 + core}, device_id_type=MESH,
        )

    def compute(i):
        d, p = steps[i]
        there = flip(chip, d, chips)
        for k, dst in ((there * 2 + 1 - core, core_src), (there * 2 + core, own)):
            dst[i, 0:upper, :] = grad_of(k, p).astype(dst.dtype)
            for j in range(side * p):
                dst[i, upper:upper + lower, j * bins:(j + 1) * bins] = out_rows(k, j).astype(dst.dtype)
            if dst is core_src:
                core_copy(i).start()

    def pass_on(i):
        d, p = steps[i]
        core_copy(i).wait()
        size_i = size(i)
        value = own[i, 0:size_i] + core_got[i, 0:size_i].astype(F32)
        if d == 0:
            own[i, 0:size_i] = value
            return
        if relay and (d, p) in ((1, 1), (2, 0)):
            came = steps.index((3, p))
            chip_copy(came).wait_recv()
            value = value + chip_got[came, 0:size_i].astype(F32)
        chip_src[i, 0:size_i] = value.astype(BF16)
        chip_copy(i).start()

    last = len(steps) - 1
    late = [i for i in range(last + 1) if relay and steps[i] in ((1, 1), (2, 0))]
    back(0)
    for i in range(last + 1):
        if i == 1:
            back(1)
            gout[...] = jnp.dot(d_logits_t, hid[rows:rows + slots, :], preferred_element_type=F32).T
        compute(i)
        if i > 0 and i - 1 not in late:
            pass_on(i - 1)
    pass_on(last)
    for i in late:
        pass_on(i)

    for i in range(last - 1):
        d, p = steps[i]
        if relayed(d):
            chip_copy(i).wait_send()
            continue
        chip_copy(i).wait()
        if i not in late:
            size_i = size(i)
            own[last - 1 + p, 0:size_i] = own[last - 1 + p, 0:size_i] + chip_got[i, 0:size_i].astype(F32)
    for p in range(2):
        size_p = size(last - 1 + p)
        total = own[last - 1 + p, 0:size_p]
        for i in late:
            if steps[i][1] == p:
                total = total + chip_got[i, 0:size_p].astype(F32)
        tot_ref[p, 0:size_p] = total
    for d in range(1, n):
        rep_copy(d, me).wait_send()


def steps_of(chips):
    if chips == 4:
        return [(3, 0), (3, 1), (1, 0), (2, 1), (1, 1), (2, 0), (0, 0), (0, 1)], True
    return [(d, p) for d in range(chips - 1, -1, -1) for p in range(2)], False


def unpack(side, tgt_in, tot, tgt_ref, gin_ref, gout_ref):
    upper, lower = gin_ref.shape[1] // 2, gout_ref.shape[0] // side
    bins = gout_ref.shape[1]
    tgt_ref[...] = tgt_in[...]
    for p in range(2):
        gin_ref[:, p * upper:(p + 1) * upper] = tot[p, 0:upper, :].T
    for j in range(side):
        gout_ref[j * lower:(j + 1) * lower, :] = tot[1, upper:upper + lower, j * bins:(j + 1) * bins]


def shards(
    members, n,
    cur_states, buffer, fetch_rows, fetch_counts, actions, rewards, terminal, mc_return, w_in, w_out
):
    slots, width = cur_states.shape
    rows = buffer.shape[0]
    head, bins = w_out.shape[1:]
    cap = fetch_rows.shape[2]
    chips = n // 2
    share = width // n
    first = slots * 3 // 8 // 128 * 128
    side = share // bins
    packed = head // 2 + head // n // side
    count = len(steps_of(chips)[0])
    parts = 4
    vmem, hbm = pl.BlockSpec(memory_space=pltpu.VMEM), pl.BlockSpec(memory_space=pl.ANY)
    dma = pltpu.SemaphoreType.DMA
    targets, totals = pl.pallas_call(
        functools.partial(kernel, n, members, first, parts),
        out_shape=(
            jax.ShapeDtypeStruct((1, slots), F32),
            jax.ShapeDtypeStruct((2, packed, share), F32),
        ),
        in_specs=[hbm, hbm, vmem, pl.BlockSpec(memory_space=pltpu.SMEM), vmem, vmem, vmem, vmem, hbm, vmem],
        out_specs=(vmem, vmem),
        scratch_shapes=[
            pltpu.VMEM((rows + slots, width), BF16),
            pltpu.VMEM((rows + slots, head), F32),
            pltpu.VMEM((width, head), BF16),
            pltpu.VMEM((bins, head), BF16),
            pltpu.VMEM((rows + slots, head), BF16),
            pltpu.VMEM((head, slots), F32),
            pltpu.VMEM((8, slots), F32),
            pltpu.VMEM((head, slots), BF16),
            pltpu.VMEM((head, bins), F32),
            pltpu.VMEM((8, rows), F32),
            pltpu.VMEM((members - 1, 8, rows), F32),
            pltpu.VMEM((n, 8, cap), F32),
            pltpu.VMEM((n, 8, cap), F32),
            pltpu.VMEM((count, packed, share), F32),
            pltpu.VMEM((count, packed, share), BF16),
            pltpu.VMEM((count, packed, share), BF16),
            pltpu.VMEM((count - 2, packed, share), BF16),
            pltpu.VMEM((count - 2, packed, share), BF16),
            dma((2 * parts,)), dma((parts + 1,)),
            dma((members - 1,)), dma((members - 1,)),
            dma((n - 1,)), dma((n,)),
            dma((count,)), dma((count,)),
            dma((count - 2,)), dma((count - 2,)),
        ],
        compiler_params=pltpu.CompilerParams(
            collective_id=0, has_side_effects=True, vmem_limit_bytes=60 * 1024 * 1024
        ),
    )(
        cur_states, buffer, fetch_rows[0], fetch_counts,
        actions.reshape(1, slots), rewards.reshape(1, slots), terminal.reshape(1, slots), mc_return.reshape(1, slots),
        w_in[0], w_out[0],
    )
    targets, grad_first, grad_second = pl.pallas_call(
        functools.partial(unpack, side),
        out_shape=(
            jax.ShapeDtypeStruct((1, slots), F32),
            jax.ShapeDtypeStruct((share, head), F32),
            jax.ShapeDtypeStruct((head // n, bins), F32),
        ),
        in_specs=[vmem, vmem],
        out_specs=(vmem, vmem, vmem),
        compiler_params=pltpu.CompilerParams(vmem_limit_bytes=60 * 1024 * 1024),
    )(targets, totals)
    return targets.reshape(slots), grad_first[None], grad_second[None]


def solution(mesh):
    placed = (
        P("rep", None),
        P("rep", None),
        P("rep", None, None),
        P(),
        P("rep"),
        P("rep"),
        P("rep"),
        P("rep"),
        P("ens", None, None),
        P("ens", None, None),
    )
    return jax.shard_map(
        functools.partial(shards, mesh.shape["ens"], mesh.shape["rep"]),
        mesh=mesh,
        in_specs=placed,
        out_specs=(P("rep"), P("ens", "rep", None), P("ens", "rep", None)),
        check_vma=False,
    )
```

```python
import functools

import jax
import jax.numpy as jnp
from jax import lax
from jax.experimental import pallas as pl
from jax.experimental.pallas import tpu as pltpu
from jax.sharding import PartitionSpec as P

F32 = jnp.float32
BF16 = jnp.bfloat16
MESH = pl.DeviceIdType.MESH


def flip(value, bits, size):
    out, base = 0, 1
    while base < size:
        out = out + ((value // base + (bits // base) % 2) % 2) * base
        base *= 2
    return out


def kernel(
    n, members, tile, parts,
    cur_hbm, buf_hbm, fetch_ref, counts_ref, act_ref, rew_ref, term_ref, mc_ref, win_hbm, wout_ref,
    tgt_ref, tot_ref,
    cur, buf, win, wout_t, hid, slope_t, tk, dh_t, gout, mine, ens_got, serve, got,
    own, core_src, core_got, chip_src, chip_got,
    in_sem, cur_sem, ens_ss, ens_rs, rep_ss, rep_rs, core_ss, core_rs, chip_ss, chip_rs,
):
    me, member = lax.axis_index("rep"), lax.axis_index("ens")
    slots, width = cur.shape
    head, bins = wout_ref.shape
    cap = fetch_ref.shape[1]
    rows = buf.shape[0]
    tiles = slots // tile
    chips = n // 2
    chip, core = me // 2, me % 2
    share = width // n
    side = share // bins
    upper, lower = head // 2, head // n // side
    steps, relay = steps_of(chips)

    def relayed(d):
        return relay and d == 3

    depth = width // parts

    def load_win(k):
        part = slice(k * depth, (k + 1) * depth)
        return pltpu.make_async_copy(win_hbm.at[part], win.at[part], in_sem.at[2 * k])

    def load_buf(k):
        part = slice(k * depth, (k + 1) * depth)
        return pltpu.make_async_copy(buf_hbm.at[:, part], buf.at[:, part], in_sem.at[2 * k + 1])

    for k in range(parts):
        load_win(k).start()
        load_buf(k).start()

    def load_cur(i):
        part = pl.ds(pl.multiple_of(i * tile, tile), tile)
        return pltpu.make_async_copy(cur_hbm.at[part], cur.at[part], cur_sem.at[i])

    barrier = pltpu.get_barrier_semaphore()
    for d in range(1, members):
        pl.semaphore_signal(barrier, inc=1, device_id={"ens": (member + d) % members}, device_id_type=MESH)
    for d in range(1, n):
        pl.semaphore_signal(barrier, inc=1, device_id={"rep": (me + d) % n}, device_id_type=MESH)

    wout_t[...] = wout_ref[...].astype(F32).T.astype(BF16)
    counted = jnp.int32(0)
    for a in range(n):
        for b in range(n):
            counted = counted + counts_ref[a, b]
    gain = 65536.0 / jnp.full((1, cap), counted, jnp.int32).astype(F32)

    def logits_of(hidden):
        return lax.dot_general(
            wout_t[...], hidden, (((1,), (1,)), ((), ())), preferred_element_type=F32
        )

    pre = None
    for k in range(parts):
        load_win(k).wait()
        load_buf(k).wait()
        if k == min(1, parts - 1):
            for i in range(tiles):
                load_cur(i).start()
        part = slice(k * depth, (k + 1) * depth)
        term = jnp.dot(buf[:, part], win[part, :], preferred_element_type=F32)
        pre = term if pre is None else pre + term
    hidden = (pre * jax.nn.sigmoid(pre)).astype(BF16)
    best = jnp.max(logits_of(hidden), axis=0, keepdims=True)
    mine[...] = jnp.broadcast_to(best, mine.shape)
    pl.semaphore_wait(barrier, members - 1 + n - 1)

    def ens_copy(d):
        return pltpu.make_async_remote_copy(
            src_ref=mine, dst_ref=ens_got.at[d - 1], send_sem=ens_ss.at[d - 1], recv_sem=ens_rs.at[d - 1],
            device_id={"ens": (member + d) % members}, device_id_type=MESH,
        )

    for d in range(1, members):
        ens_copy(d).start()

    def forward(i, carry):
        load_cur(i).wait()
        part = pl.ds(pl.multiple_of(i * tile, tile), tile)
        pre = jnp.dot(cur[part, :], win[...], preferred_element_type=F32)
        sig = jax.nn.sigmoid(pre)
        hidden = (pre * sig).astype(BF16)
        hid[part, :] = hidden
        slope_t[:, part] = (sig * (1.0 + pre * (1.0 - sig))).T
        logits = logits_of(hidden)
        chosen = lax.broadcasted_iota(jnp.int32, (bins, tile), 0) == act_ref[0:1, part]
        tk[0:1, part] = jnp.sum(jnp.where(chosen, logits, 0.0), axis=0, keepdims=True)
        return carry

    lax.fori_loop(0, tiles // 2, forward, 0)

    floor = mine[0:1, :]
    for d in range(1, members):
        ens_copy(d).wait()
        floor = jnp.minimum(floor, ens_got[d - 1, 0:1, :])
    eye = lax.broadcasted_iota(jnp.int32, (rows, rows), 0) == lax.broadcasted_iota(jnp.int32, (rows, rows), 1)
    floor_col = jnp.sum(jnp.where(eye, jnp.broadcast_to(floor, (rows, rows)), 0.0), axis=1, keepdims=True)
    row_ids = lax.broadcasted_iota(jnp.int32, (rows, cap), 0)
    for r in range(n):
        hit = row_ids == fetch_ref[r:r + 1, :]
        served = jnp.sum(jnp.where(hit, jnp.broadcast_to(floor_col, (rows, cap)), 0.0), axis=0, keepdims=True)
        serve[r] = jnp.broadcast_to(served, serve.shape[1:])

    def rep_copy(d, slot):
        dst = (me + d) % n
        return pltpu.make_async_remote_copy(
            src_ref=serve.at[dst], dst_ref=got.at[slot], send_sem=rep_ss.at[d - 1], recv_sem=rep_rs.at[slot],
            device_id={"rep": dst}, device_id_type=MESH,
        )

    for d in range(1, n):
        rep_copy(d, me).start()
    got[me] = serve[me]

    lax.fori_loop(tiles // 2, tiles, forward, 0)

    for d in range(1, n):
        rep_copy(d, (me + n - d) % n).wait_recv()
    place = lax.broadcasted_iota(jnp.int32, (1, cap), 1)
    bin_ids = lax.broadcasted_iota(jnp.int32, (bins, cap), 0)
    pieces = []
    for o in range(n):
        part = slice(o * cap, (o + 1) * cap)
        used = jnp.where(place < counts_ref[o, me], 1.0, 0.0)
        bootstrap = jnp.maximum(jax.nn.sigmoid(got[o, 0:1, :]), mc_ref[0:1, part])
        target = rew_ref[0:1, part] + 0.98 * (1.0 - term_ref[0:1, part].astype(F32)) * bootstrap
        tgt_ref[0:1, part] = used * target
        taken = jax.nn.sigmoid(tk[0:1, part])
        errors = used * 2.0 * (taken - target) * taken * (1.0 - taken) * gain
        pieces.append(jnp.where(bin_ids == act_ref[0:1, part], errors, 0.0).astype(BF16))
    d_logits_t = jnp.concatenate(pieces, axis=1)

    def back(p):
        part = slice(p * upper, (p + 1) * upper)
        back_t = jnp.dot(wout_ref[part, :], d_logits_t, preferred_element_type=F32)
        dh_t[part, :] = (back_t * slope_t[part, :]).astype(BF16)

    def grad_of(k, p):
        cols = pl.ds(pl.multiple_of(k * share, share), share)
        return jnp.dot(dh_t[p * upper:(p + 1) * upper, :], cur[:, cols], preferred_element_type=F32)

    def out_rows(k, j):
        return gout[pl.ds(pl.multiple_of((k * side + j) * lower, lower), lower), :]

    def size(i):
        return upper + lower * steps[i][1]

    def core_copy(i):
        return pltpu.make_async_remote_copy(
            src_ref=core_src.at[i, 0:size(i)], dst_ref=core_got.at[i, 0:size(i)], send_sem=core_ss.at[i], recv_sem=core_rs.at[i],
            device_id={"rep": chip * 2 + 1 - core}, device_id_type=MESH,
        )

    def chip_copy(i):
        d, p = steps[i]
        there = flip(chip, p + 1 if relayed(d) else d, chips)
        return pltpu.make_async_remote_copy(
            src_ref=chip_src.at[i, 0:size(i)], dst_ref=chip_got.at[i, 0:size(i)], send_sem=chip_ss.at[i], recv_sem=chip_rs.at[i],
            device_id={"rep": there * 2 + core}, device_id_type=MESH,
        )

    def compute(i):
        d, p = steps[i]
        there = flip(chip, d, chips)
        for k, dst in ((there * 2 + 1 - core, core_src), (there * 2 + core, own)):
            dst[i, 0:upper, :] = grad_of(k, p).astype(dst.dtype)
            for j in range(side * p):
                dst[i, upper:upper + lower, j * bins:(j + 1) * bins] = out_rows(k, j).astype(dst.dtype)
            if dst is core_src:
                core_copy(i).start()
                if i > 1 and i - 1 not in late:
                    pass_on(i - 1)

    def pass_on(i):
        d, p = steps[i]
        core_copy(i).wait()
        size_i = size(i)
        value = own[i, 0:size_i] + core_got[i, 0:size_i].astype(F32)
        if d == 0:
            own[i, 0:size_i] = value
            return
        if relay and (d, p) in ((1, 1), (2, 0)):
            came = steps.index((3, p))
            chip_copy(came).wait_recv()
            value = value + chip_got[came, 0:size_i].astype(F32)
        chip_src[i, 0:size_i] = value.astype(BF16)
        chip_copy(i).start()

    last = len(steps) - 1
    late = [i for i in range(last + 1) if relay and steps[i] in ((1, 1), (2, 0))]
    back(0)
    for i in range(last + 1):
        if i == 1:
            back(1)
            gout[...] = jnp.dot(d_logits_t, hid[...], preferred_element_type=F32).T
            pass_on(0)
        compute(i)
    pass_on(last)
    for i in late:
        pass_on(i)

    for i in range(last - 1):
        d, p = steps[i]
        if relayed(d):
            chip_copy(i).wait_send()
            continue
        chip_copy(i).wait()
        if i not in late:
            size_i = size(i)
            own[last - 1 + p, 0:size_i] = own[last - 1 + p, 0:size_i] + chip_got[i, 0:size_i].astype(F32)
    for p in range(2):
        size_p = size(last - 1 + p)
        total = own[last - 1 + p, 0:size_p]
        for i in late:
            if steps[i][1] == p:
                total = total + chip_got[i, 0:size_p].astype(F32)
        tot_ref[p, 0:size_p] = total
    for d in range(1, n):
        rep_copy(d, me).wait_send()


def steps_of(chips):
    if chips == 4:
        return [(3, 0), (3, 1), (1, 0), (2, 1), (1, 1), (2, 0), (0, 0), (0, 1)], True
    return [(d, p) for d in range(chips - 1, -1, -1) for p in range(2)], False


def unpack(side, tgt_in, tot, tgt_ref, gin_ref, gout_ref):
    upper, lower = gin_ref.shape[1] // 2, gout_ref.shape[0] // side
    bins = gout_ref.shape[1]
    tgt_ref[...] = tgt_in[...]
    for p in range(2):
        gin_ref[:, p * upper:(p + 1) * upper] = tot[p, 0:upper, :].T
    for j in range(side):
        gout_ref[j * lower:(j + 1) * lower, :] = tot[1, upper:upper + lower, j * bins:(j + 1) * bins]


def shards(
    members, n,
    cur_states, buffer, fetch_rows, fetch_counts, actions, rewards, terminal, mc_return, w_in, w_out
):
    slots, width = cur_states.shape
    rows = buffer.shape[0]
    head, bins = w_out.shape[1:]
    cap = fetch_rows.shape[2]
    chips = n // 2
    share = width // n
    tile = min(256, slots // 2)
    side = share // bins
    packed = head // 2 + head // n // side
    count = len(steps_of(chips)[0])
    parts = 4
    vmem, hbm = pl.BlockSpec(memory_space=pltpu.VMEM), pl.BlockSpec(memory_space=pl.ANY)
    dma = pltpu.SemaphoreType.DMA
    targets, totals = pl.pallas_call(
        functools.partial(kernel, n, members, tile, parts),
        out_shape=(
            jax.ShapeDtypeStruct((1, slots), F32),
            jax.ShapeDtypeStruct((2, packed, share), F32),
        ),
        in_specs=[hbm, hbm, vmem, pl.BlockSpec(memory_space=pltpu.SMEM), vmem, vmem, vmem, vmem, hbm, vmem],
        out_specs=(vmem, vmem),
        scratch_shapes=[
            pltpu.VMEM((slots, width), BF16),
            pltpu.VMEM((rows, width), BF16),
            pltpu.VMEM((width, head), BF16),
            pltpu.VMEM((bins, head), BF16),
            pltpu.VMEM((slots, head), BF16),
            pltpu.VMEM((head, slots), F32),
            pltpu.VMEM((8, slots), F32),
            pltpu.VMEM((head, slots), BF16),
            pltpu.VMEM((head, bins), F32),
            pltpu.VMEM((8, rows), F32),
            pltpu.VMEM((members - 1, 8, rows), F32),
            pltpu.VMEM((n, 8, cap), F32),
            pltpu.VMEM((n, 8, cap), F32),
            pltpu.VMEM((count, packed, share), F32),
            pltpu.VMEM((count, packed, share), BF16),
            pltpu.VMEM((count, packed, share), BF16),
            pltpu.VMEM((count - 2, packed, share), BF16),
            pltpu.VMEM((count - 2, packed, share), BF16),
            dma((2 * parts,)), dma((slots // tile,)),
            dma((members - 1,)), dma((members - 1,)),
            dma((n - 1,)), dma((n,)),
            dma((count,)), dma((count,)),
            dma((count - 2,)), dma((count - 2,)),
        ],
        compiler_params=pltpu.CompilerParams(
            collective_id=0, has_side_effects=True, vmem_limit_bytes=60 * 1024 * 1024
        ),
    )(
        cur_states, buffer, fetch_rows[0], fetch_counts,
        actions.reshape(1, slots), rewards.reshape(1, slots), terminal.reshape(1, slots), mc_return.reshape(1, slots),
        w_in[0], w_out[0],
    )
    targets, grad_first, grad_second = pl.pallas_call(
        functools.partial(unpack, side),
        out_shape=(
            jax.ShapeDtypeStruct((1, slots), F32),
            jax.ShapeDtypeStruct((share, head), F32),
            jax.ShapeDtypeStruct((head // n, bins), F32),
        ),
        in_specs=[vmem, vmem],
        out_specs=(vmem, vmem, vmem),
        compiler_params=pltpu.CompilerParams(vmem_limit_bytes=60 * 1024 * 1024),
    )(targets, totals)
    return targets.reshape(slots), grad_first[None], grad_second[None]


def solution(mesh):
    placed = (
        P("rep", None),
        P("rep", None),
        P("rep", None, None),
        P(),
        P("rep"),
        P("rep"),
        P("rep"),
        P("rep"),
        P("ens", None, None),
        P("ens", None, None),
    )
    return jax.shard_map(
        functools.partial(shards, mesh.shape["ens"], mesh.shape["rep"]),
        mesh=mesh,
        in_specs=placed,
        out_specs=(P("rep"), P("ens", "rep", None), P("ens", "rep", None)),
        check_vma=False,
    )
```
